512 devices in a mesh: row: 16 (over y, core), col: 32 (over z, x).
Axes of the slice: x: 4, y: 8, z: 8, core: 2. Of those that a mesh axis runs over, the one named last changes fastest.
Arguments:
- covariance: float32 [16384, 16384], P('row', 'col'), may hold values from -80 to 80, as said below
Outputs:
- factored: float32 [16384, 16384], P('row', 'col')
The draws below stay inside these ranges and needn't reach their ends.
Inputs may be any that keep to these rules, and one draw needn't show every extreme that they name: covariance holds, in the storage order of the first step, a symmetric positive definite matrix whose eigenvalues are at least a quarter of its smallest diagonal entry.
All inputs are finite; a program needn't handle non-finite values.
Results may differ from the reference program's by a relative error of at most 0.0003.
Values sent between devices are 32-bit elements; how exact they have to be, the bound alone decides.
No kernel may reach another device: no remote copies, remote signals or barrier semaphores. Data moves between devices by JAX's collectives and lax.ppermute only.
A program may use at most 64 MiB of HBM per device.

```python
import jax
import jax.numpy as jnp
from jax import lax

ORDER = 16384
NB = 512
STEPS = 1
N_ROW = 16
N_COL = 32


def draw_covariance(key, part):
    key = jax.random.fold_in(key, 11)
    key_noise, key_var, key_common = jax.random.split(key, 3)
    count = ORDER
    spread = 0.25 / count ** 0.5
    noise = jax.random.normal(key_noise, (count, count), jnp.float32)
    variance = jnp.exp(jax.random.uniform(key_var, (count,), jnp.float32, 0.0, jnp.log(10.0)))
    common = jax.random.uniform(key_common, (count,), jnp.float32, 0.5, 1.5)
    weight = 0.3
    symmetric = (noise + noise.T) * (spread * 0.70710678)
    scale = jnp.sqrt(variance)
    corr = jnp.eye(count, dtype=jnp.float32) + symmetric + weight * common[:, None] * common[None, :]
    sigma = scale[:, None] * corr * scale[None, :]
    whole = jnp.arange(count, dtype=jnp.int32)
    local_rows = count // N_ROW
    local_cols = count // N_COL
    grow = (whole % local_rows // NB * N_ROW + whole // local_rows) * NB + whole % local_rows % NB
    gcol = (whole % local_cols // NB * N_COL + whole // local_cols) * NB + whole % local_cols % NB
    return sigma[grow][:, gcol]


def setup_inputs(seed: int = 0) -> dict:
    arg_keys = jax.random.split(jax.random.key(seed), 2)
    return {
        "covariance": draw_covariance(jax.random.fold_in(arg_keys[1], 71), 0),
    }


HIGH = lax.Precision.HIGHEST

def stored_spot(count, tile, groups):
    whole = jnp.arange(count, dtype=jnp.int32)
    tiles = whole // tile
    offset = whole % tile
    return tiles % groups * (count // groups) + tiles // groups * tile + offset

def global_spot(count, tile, groups):
    whole = jnp.arange(count, dtype=jnp.int32)
    local = count // groups
    group_id = whole // local
    inside = whole % local
    return (inside // tile * groups + group_id) * tile + inside % tile

def reference(covariance):
    sigma = covariance[stored_spot(ORDER, NB, N_ROW)][:, stored_spot(ORDER, NB, N_COL)]
    rows = jnp.arange(ORDER, dtype=jnp.int32)
    for step in range(STEPS):
        low = step * NB
        high = low + NB
        factor = jnp.linalg.cholesky(sigma[low:high, low:high])
        inverse = lax.linalg.triangular_solve(factor, jnp.eye(NB, dtype=sigma.dtype), left_side=True, lower=True)
        solved = lax.dot_general(sigma[:, low:high], inverse, (((1,), (1,)), ((), ())), precision=HIGH)
        lower = jnp.where((rows >= high)[:, None], solved, jnp.zeros_like(solved))
        lower = lower.at[low:high].set(factor)
        below = lower[high:]
        trail = sigma[high:, high:] - lax.dot_general(below, below, (((1,), (1,)), ((), ())), precision=HIGH)
        sigma = sigma.at[:, low:high].set(lower)
        sigma = sigma.at[:high, high:].set(jnp.zeros((high, ORDER - high), sigma.dtype))
        sigma = sigma.at[high:, high:].set(trail)
    return sigma[global_spot(ORDER, NB, N_ROW)][:, global_spot(ORDER, NB, N_COL)]
```

```python
import functools

import jax
import jax.numpy as jnp
from jax import lax
from jax.experimental import pallas as pl
from jax.experimental.pallas import tpu as pltpu
from jax.sharding import Mesh
from jax.sharding import PartitionSpec as P

NB = 512
BK = 128
SUB = 8
CHUNK = 256
HIGH = lax.Precision.HIGHEST


def _rows(value, m):
    return jnp.broadcast_to(value[m : m + 1, :], (SUB, BK))


def _lanes(value, m):
    return jnp.broadcast_to(value[:, m : m + 1], (SUB, BK))


def _small_inverse(rows):
    lane = lax.broadcasted_iota(jnp.int32, (SUB, BK), 1)
    sub = lax.broadcasted_iota(jnp.int32, (SUB, BK), 0)
    rows = list(rows)
    n = len(rows)
    out = []
    for k in range(n):
        base = SUB * k
        pivot = (lane >= base) & (lane < base + SUB)
        p = [_rows(rows[k], m) for m in range(SUB)]
        c = [[_lanes(p[m], base + l) if l >= m else None for l in range(SUB)] for m in range(SUB)]
        p = [
            jnp.where(pivot, jnp.where(lane == base + m, 1.0, 0.0), p[m]) for m in range(SUB)
        ]
        if k + 1 < n:
            g = [_lanes(rows[k + 1], base + m) for m in range(SUB)]
            ahead = jnp.where(pivot, 0.0, rows[k + 1])
        f = [[None] * SUB for _ in range(SUB)]
        inv = []
        for j in range(SUB):
            inv.append(pl.reciprocal(c[j][j], approx=True))
            for l in range(j + 1, SUB):
                f[j][l] = c[j][l] * inv[j]
                for l2 in range(l, SUB):
                    c[l][l2] = c[l][l2] - f[j][l] * c[j][l2]
            for l in range(j + 1, SUB):
                p[l] = p[l] - f[j][l] * p[j]
            if k + 1 < n:
                h = g[j] * inv[j]
                ahead = ahead - h * p[j]
                for l in range(j + 1, SUB):
                    g[l] = g[l] - h * c[j][l]
        done = p[0] * lax.rsqrt(c[0][0])
        for m in range(1, SUB):
            done = jnp.where(sub == m, p[m] * lax.rsqrt(c[m][m]), done)
        out.append(jnp.where(lane <= sub + base, done, 0.0))
        if k + 1 < n:
            rows[k + 1] = ahead
        if k + 2 < n:
            s = [p[m] * inv[m] for m in range(SUB)]
            for l in range(SUB - 1, 0, -1):
                for j in range(l):
                    s[j] = s[j] - f[j][l] * s[l]
            for i in range(k + 2, n):
                parts = [_lanes(rows[i], base + m) * s[m] for m in range(SUB)]
                while len(parts) > 1:
                    parts = [a + b for a, b in zip(parts[::2], parts[1::2])]
                rows[i] = jnp.where(pivot, 0.0, rows[i]) - parts[0]
    return out


def _dot(a, b):
    return lax.dot_general(
        a,
        b,
        (((1,), (0,)), ((), ())),
        precision=HIGH,
        preferred_element_type=jnp.float32,
    )


def _eliminate(k, v_ref):
    here = slice(k * BK, (k + 1) * BK)
    rows = [v_ref[k * BK + SUB * i : k * BK + SUB * (i + 1), here] for i in range(BK // SUB)]
    small = jnp.concatenate(_small_inverse(rows), axis=0)
    v_ref[here, :] = _dot(small, v_ref[here, :])
    v_ref[here, here] = small
    for i in range(k + 1, NB // BK):
        there = slice(i * BK, (i + 1) * BK)
        v_ref[there, here] = jnp.zeros((BK, BK), jnp.float32)
        v_ref[there, :] -= _dot(v_ref[here, there].T, v_ref[here, :])


def _first_kernel(here_ref, mine_ref, other_ref, v_ref):
    half = NB // 2

    @pl.when(here_ref[2] == 0)
    def _():
        v_ref[:half, :] = mine_ref[...]
        v_ref[half:, :] = other_ref[...]

    @pl.when(here_ref[2] != 0)
    def _():
        v_ref[:half, :] = other_ref[...]
        v_ref[half:, :] = mine_ref[...]

    _eliminate(0, v_ref)


def _next_kernel(k, old_ref, v_ref):
    v_ref[...] = old_ref[...]
    _eliminate(k, v_ref)


def _handing_kernel(old_ref, _, v_ref, __):
    _next_kernel(1, old_ref, v_ref)


def factor_inverse(here, mine, other, own):
    vmem = pl.BlockSpec(memory_space=pltpu.VMEM)
    rest = dict(
        out_shape=jax.ShapeDtypeStruct((NB, NB), jnp.float32),
        out_specs=vmem,
        compiler_params=pltpu.CompilerParams(vmem_limit_bytes=24 * 2**20),
        cost_estimate=pl.CostEstimate(
            flops=8 * 10**9, bytes_accessed=8 * NB * NB, transcendentals=NB
        ),
    )
    state = pl.pallas_call(
        _first_kernel,
        in_specs=[pl.BlockSpec(memory_space=pltpu.SMEM), vmem, vmem],
        name="factor_0",
        **rest,
    )(here, mine, other)
    handed = dict(
        rest,
        out_shape=(rest["out_shape"], jax.ShapeDtypeStruct(own.shape, own.dtype)),
        out_specs=(vmem, pl.BlockSpec(memory_space=pl.ANY)),
        input_output_aliases={1: 1},
    )
    for k in range(1, NB // BK):
        if k == 1:
            state, own = pl.pallas_call(
                _handing_kernel,
                in_specs=[vmem, pl.BlockSpec(memory_space=pl.ANY)],
                name="factor_1",
                **handed,
            )(state, own)
        else:
            state = pl.pallas_call(
                functools.partial(_next_kernel, k), in_specs=[vmem], name=f"factor_{k}", **rest
            )(state)
    return state, own


def _split(value):
    top = value.astype(jnp.bfloat16)
    return top, (value - top.astype(jnp.float32)).astype(jnp.bfloat16)


def _dot3(a, b, dims):
    return sum(
        lax.dot_general(x, y, (dims, ((), ())), preferred_element_type=jnp.float32)
        for x, y in ((a[1], b[0]), (a[0], b[1]), (a[0], b[0]))
    )


def _update_kernel(
    here_ref, state_ref, own_ref, back_ref, top_ref, low_ref, ahead_ref, tile_ref, inverse_ref,
    o_ref, panel_ref, inv_ref, mirror_ref,
):
    row, col, x = here_ref[0], here_ref[1], here_ref[3]
    i = pl.program_id(0)
    first = pl.multiple_of(i * CHUNK, CHUNK)
    half = CHUNK // 2

    @pl.when(i == 0)
    def _():
        for k in range(NB // BK):
            here = slice(k * BK, (k + 1) * BK)
            wide = inverse_ref[here, :]
            lane = lax.broadcasted_iota(jnp.int32, wide.shape, 1)
            top, low = _split(jnp.where(lane < (k + 1) * BK, wide, 0.0))
            inv_ref[0, here, :] = top
            inv_ref[1, here, :] = low

        mirror = _split(_dot3((inv_ref[0], inv_ref[1]), _split(tile_ref[...]), ((1,), (0,))))
        mirror_ref[0] = mirror[0]
        mirror_ref[1] = mirror[1]

    turn = lax.rem(x + 4 - i, 4)
    for j, part in ((0, own_ref), (1, back_ref), (3, ahead_ref)):

        @pl.when(turn == j)
        def _():
            panel_ref[...] = part[...]

    @pl.when(turn == 2)
    def _():
        panel_ref[:half, :] = top_ref[...]
        panel_ref[half:, :] = low_ref[...]

    solved = _dot3(_split(panel_ref[...]), (inv_ref[0], inv_ref[1]), ((1,), (1,)))
    top = (row == 0) & (first < NB)

    @pl.when(col == 0)
    def _():
        r = lax.broadcasted_iota(jnp.int32, solved.shape, 0) + first
        c = lax.broadcasted_iota(jnp.int32, solved.shape, 1)
        o_ref[...] = jnp.where(top & (c > r), 0.0, solved)

    @pl.when(col != 0)
    def _():
        new = state_ref[...] - _dot3(_split(solved), (mirror_ref[0], mirror_ref[1]), ((1,), (0,)))
        o_ref[...] = jnp.where(top, 0.0, new)


def update(here, state, panel, mirror, inverse):
    block = pl.BlockSpec((CHUNK, NB), lambda i: (i, 0))
    vmem = pl.BlockSpec(memory_space=pltpu.VMEM)
    return pl.pallas_call(
        _update_kernel,
        grid=(state.shape[0] // CHUNK,),
        out_shape=jax.ShapeDtypeStruct(state.shape, jnp.float32),
        in_specs=[pl.BlockSpec(memory_space=pltpu.SMEM), block] + [vmem] * 7,
        out_specs=block,
        scratch_shapes=[
            pltpu.VMEM((CHUNK, NB), jnp.float32),
            pltpu.VMEM((2, NB, NB), jnp.bfloat16),
            pltpu.VMEM((2, NB, NB), jnp.bfloat16),
        ],
        compiler_params=pltpu.CompilerParams(vmem_limit_bytes=40 * 2**20),
        cost_estimate=pl.CostEstimate(
            flops=30 * NB**3, bytes_accessed=32 * NB * NB, transcendentals=0
        ),
        name="update",
    )(here, state, *panel, mirror, inverse)


def send_parts(value, axis, parts):
    size = value.shape[0] // parts
    return lax.all_to_all(value.reshape(parts, size, value.shape[1]), axis, 0, 0)[0]


def gather(value, axis, parts):
    copies = jnp.broadcast_to(value[None], (parts,) + value.shape)
    return lax.all_to_all(copies, axis, 0, 0).reshape(-1, value.shape[1])


def swap_cores(value):
    return lax.ppermute(value, "core", [(0, 1), (1, 0)])


def body(covariance):
    ny, nz, nx = (lax.axis_size(axis) for axis in ("y", "z", "x"))
    core, x, y, z = (lax.axis_index(axis) for axis in ("core", "x", "y", "z"))
    half = NB // 2
    here = jnp.stack([y * 2 + core, z * nx + x, core, x]).astype(jnp.int32)

    tile = covariance[:NB]
    mine = jnp.where(core == 0, tile[:half], swap_cores(tile[half:]))

    part = send_parts(mine, ("z", "x"), nz * nx)
    part = gather(part, "y", ny)[: part.shape[0]]
    diagonal = gather(part, ("z", "x"), nz * nx)

    size = covariance.shape[0] // nx
    quarter = jnp.where(x == 0, covariance[:size], 0.0)
    for i in range(1, nx):
        quarter = quarter + lax.ppermute(
            covariance[i * size : (i + 1) * size], ("z", "x"), [(0, i)]
        )
    spread = lax.ppermute(quarter, "z", [(0, 3)]) + lax.ppermute(quarter, "z", [(0, 5)])
    spread = jnp.where(z == 0, quarter, spread)
    own = lax.ppermute(spread, "z", [(0, 1), (3, 4), (5, 6)])
    own = own + lax.ppermute(spread, "z", [(0, 7), (3, 2)])
    own = jnp.where((z == 0) | (z == 3) | (z == 5), spread, own)

    inverse, own = factor_inverse(here, diagonal, swap_cores(diagonal), own)

    ring = [(i, (i + 1) % nx) for i in range(nx)]
    back_ring = [(j, i) for i, j in ring]
    back = lax.ppermute(own, "x", ring)
    ahead = lax.ppermute(own, "x", back_ring)
    top = lax.ppermute(back[: size // 2], "x", ring)
    low = lax.ppermute(ahead[size // 2 :], "x", back_ring)

    mirror = tile
    for step in (4, 2, 1):
        pairs = [(2 * i, 2 * (i + step)) for i in range(0, ny, 2 * step)]
        sent = lax.ppermute(mirror, ("y", "core"), pairs)
        mirror = jnp.where(y % (2 * step) == step, sent, mirror)
    mirror = jnp.where(core == 0, mirror, lax.ppermute(mirror, "core", [(0, 1)]))
    return update(here, covariance, (own, back, top, low, ahead), mirror, inverse)


def solution(mesh):
    fine = Mesh(mesh.devices.reshape(8, 2, 8, 4), ("y", "core", "z", "x"))
    spec = P(("y", "core"), ("z", "x"))
    return jax.shard_map(body, mesh=fine, in_specs=(spec,), out_specs=spec, check_vma=False)
```

```python
import functools

import jax
import jax.numpy as jnp
from jax import lax
from jax.experimental import pallas as pl
from jax.experimental.pallas import tpu as pltpu
from jax.sharding import Mesh
from jax.sharding import PartitionSpec as P

NB = 512
BK = 128
SUB = 8
CHUNK = 256
HIGH = lax.Precision.HIGHEST


def _rows(value, m):
    return jnp.broadcast_to(value[m : m + 1, :], (SUB, BK))


def _lanes(value, m):
    return jnp.broadcast_to(value[:, m : m + 1], (SUB, BK))


def _small_inverse(rows):
    lane = lax.broadcasted_iota(jnp.int32, (SUB, BK), 1)
    sub = lax.broadcasted_iota(jnp.int32, (SUB, BK), 0)
    rows = list(rows)
    n = len(rows)
    out = []
    for k in range(n):
        base = SUB * k
        pivot = (lane >= base) & (lane < base + SUB)
        p = [_rows(rows[k], m) for m in range(SUB)]
        c = [[_lanes(p[m], base + l) if l >= m else None for l in range(SUB)] for m in range(SUB)]
        p = [
            jnp.where(pivot, jnp.where(lane == base + m, 1.0, 0.0), p[m]) for m in range(SUB)
        ]
        if k + 1 < n:
            g = [_lanes(rows[k + 1], base + m) for m in range(SUB)]
            ahead = jnp.where(pivot, 0.0, rows[k + 1])
        f = [[None] * SUB for _ in range(SUB)]
        inv = []
        for j in range(SUB):
            inv.append(pl.reciprocal(c[j][j], approx=True))
            for l in range(j + 1, SUB):
                f[j][l] = c[j][l] * inv[j]
                for l2 in range(l, SUB):
                    c[l][l2] = c[l][l2] - f[j][l] * c[j][l2]
            for l in range(j + 1, SUB):
                p[l] = p[l] - f[j][l] * p[j]
            if k + 1 < n:
                h = g[j] * inv[j]
                ahead = ahead - h * p[j]
                for l in range(j + 1, SUB):
                    g[l] = g[l] - h * c[j][l]
        done = p[0] * lax.rsqrt(c[0][0])
        for m in range(1, SUB):
            done = jnp.where(sub == m, p[m] * lax.rsqrt(c[m][m]), done)
        out.append(jnp.where(lane <= sub + base, done, 0.0))
        if k + 1 < n:
            rows[k + 1] = ahead
        if k + 2 < n:
            s = [p[m] * inv[m] for m in range(SUB)]
            for l in range(SUB - 1, 0, -1):
                for j in range(l):
                    s[j] = s[j] - f[j][l] * s[l]
            for i in range(k + 2, n):
                parts = [_lanes(rows[i], base + m) * s[m] for m in range(SUB)]
                while len(parts) > 1:
                    parts = [a + b for a, b in zip(parts[::2], parts[1::2])]
                rows[i] = jnp.where(pivot, 0.0, rows[i]) - parts[0]
    return out


def _dot(a, b):
    return lax.dot_general(
        a,
        b,
        (((1,), (0,)), ((), ())),
        precision=HIGH,
        preferred_element_type=jnp.float32,
    )


def _eliminate(k, v_ref):
    here = slice(k * BK, (k + 1) * BK)
    rows = [v_ref[k * BK + SUB * i : k * BK + SUB * (i + 1), here] for i in range(BK // SUB)]
    small = jnp.concatenate(_small_inverse(rows), axis=0)
    v_ref[here, :] = _dot(small, v_ref[here, :])
    v_ref[here, here] = small
    for i in range(k + 1, NB // BK):
        there = slice(i * BK, (i + 1) * BK)
        v_ref[there, here] = jnp.zeros((BK, BK), jnp.float32)
        v_ref[there, :] -= _dot(v_ref[here, there].T, v_ref[here, :])


def _factor_kernel(k, old_ref, v_ref):
    v_ref[...] = old_ref[...]
    _eliminate(k, v_ref)


def factor_inverse(covariance):
    state = covariance
    for k in range(NB // BK):
        state = pl.pallas_call(
            functools.partial(_factor_kernel, k),
            grid=(1,),
            out_shape=jax.ShapeDtypeStruct((NB, NB), jnp.float32),
            in_specs=[pl.BlockSpec((NB, NB), lambda i: (0, 0))],
            out_specs=pl.BlockSpec((NB, NB), lambda i: (0, 0)),
            compiler_params=pltpu.CompilerParams(vmem_limit_bytes=24 * 2**20),
            cost_estimate=pl.CostEstimate(flops=10**6, bytes_accessed=10**5, transcendentals=NB),
            name=f"factor_{k}",
        )(state)
    return state


def _pick_kernel(which_ref, first_ref, *refs):
    *others, o_ref, sem = refs
    for i, ref in enumerate((first_ref.at[: o_ref.shape[0]], *others)):

        @pl.when(which_ref[0] == i)
        def _():
            copy = pltpu.make_async_copy(ref, o_ref, sem)
            copy.start()
            copy.wait()


def pick(which, first, *others):
    return pl.pallas_call(
        _pick_kernel,
        out_shape=jax.ShapeDtypeStruct(others[0].shape, jnp.float32),
        in_specs=[pl.BlockSpec(memory_space=pltpu.SMEM)]
        + [pl.BlockSpec(memory_space=pl.ANY)] * (1 + len(others)),
        out_specs=pl.BlockSpec(memory_space=pltpu.VMEM),
        scratch_shapes=[pltpu.SemaphoreType.DMA],
        cost_estimate=pl.CostEstimate(flops=0, bytes_accessed=10**6, transcendentals=0),
        name="pick",
    )(which.reshape(1), first, *others)


def _split(value):
    top = value.astype(jnp.bfloat16)
    return top, (value - top.astype(jnp.float32)).astype(jnp.bfloat16)


def _dot3(a, b, dims):
    return sum(
        lax.dot_general(x, y, (dims, ((), ())), preferred_element_type=jnp.float32)
        for x, y in ((a[1], b[0]), (a[0], b[1]), (a[0], b[0]))
    )


def _update_kernel(
    here_ref, state_ref, own_ref, back_ref, top_ref, low_ref, ahead_ref, tile_ref, sent_ref,
    mine_ref, other_ref, o_ref, panel_ref, whole_ref, inv_ref, mirror_ref, sem,
):
    row, col, core, x = (here_ref[j] for j in range(4))
    i = pl.program_id(0)
    first = pl.multiple_of(i * CHUNK, CHUNK)
    half = CHUNK // 2

    @pl.when(i == 0)
    def _():
        for value, ref in ((0, tile_ref), (1, sent_ref)):

            @pl.when(core == value)
            def _():
                copy = pltpu.make_async_copy(ref, whole_ref, sem)
                copy.start()
                copy.wait()

        tile = _split(whole_ref[...])
        for value, parts in ((0, (mine_ref, other_ref)), (1, (other_ref, mine_ref))):

            @pl.when(core == value)
            def _():
                for k in range(NB // BK):
                    here = slice(k * BK, (k + 1) * BK)
                    wide = parts[k // 2][(k % 2) * BK : (k % 2 + 1) * BK, :]
                    lane = lax.broadcasted_iota(jnp.int32, wide.shape, 1)
                    top, low = _split(jnp.where(lane < (k + 1) * BK, wide, 0.0))
                    inv_ref[0, here, :] = top
                    inv_ref[1, here, :] = low

        mirror = _split(_dot3((inv_ref[0], inv_ref[1]), tile, ((1,), (0,))))
        mirror_ref[0] = mirror[0]
        mirror_ref[1] = mirror[1]

    turn = lax.rem(x + 4 - i, 4)
    for j, part in ((0, own_ref), (1, back_ref), (3, ahead_ref)):

        @pl.when(turn == j)
        def _():
            panel_ref[...] = part[...]

    @pl.when(turn == 2)
    def _():
        panel_ref[:half, :] = top_ref[...]
        panel_ref[half:, :] = low_ref[...]

    solved = _dot3(_split(panel_ref[...]), (inv_ref[0], inv_ref[1]), ((1,), (1,)))
    top = (row == 0) & (first < NB)

    @pl.when(col == 0)
    def _():
        r = lax.broadcasted_iota(jnp.int32, solved.shape, 0) + first
        c = lax.broadcasted_iota(jnp.int32, solved.shape, 1)
        o_ref[...] = jnp.where(top & (c > r), 0.0, solved)

    @pl.when(col != 0)
    def _():
        new = state_ref[...] - _dot3(_split(solved), (mirror_ref[0], mirror_ref[1]), ((1,), (0,)))
        o_ref[...] = jnp.where(top, 0.0, new)


def update(here, state, panel, mirror, inverse):
    block = pl.BlockSpec((CHUNK, NB), lambda i: (i, 0))
    vmem = pl.BlockSpec(memory_space=pltpu.VMEM)
    anywhere = pl.BlockSpec(memory_space=pl.ANY)
    return pl.pallas_call(
        _update_kernel,
        grid=(state.shape[0] // CHUNK,),
        out_shape=jax.ShapeDtypeStruct(state.shape, jnp.float32),
        in_specs=[pl.BlockSpec(memory_space=pltpu.SMEM), block]
        + [vmem] * 5
        + [anywhere] * 2
        + [vmem] * 2,
        out_specs=block,
        scratch_shapes=[
            pltpu.VMEM((CHUNK, NB), jnp.float32),
            pltpu.VMEM((NB, NB), jnp.float32),
            pltpu.VMEM((2, NB, NB), jnp.bfloat16),
            pltpu.VMEM((2, NB, NB), jnp.bfloat16),
            pltpu.SemaphoreType.DMA,
        ],
        compiler_params=pltpu.CompilerParams(vmem_limit_bytes=40 * 2**20),
        cost_estimate=pl.CostEstimate(
            flops=30 * NB**3, bytes_accessed=32 * NB * NB, transcendentals=0
        ),
        name="update",
    )(here, state, *panel, *mirror, *inverse)


def send_parts(value, axis, parts):
    size = value.shape[0] // parts
    return lax.all_to_all(value.reshape(parts, size, value.shape[1]), axis, 0, 0)[0]


def gather(value, axis, parts):
    copies = jnp.broadcast_to(value[None], (parts,) + value.shape)
    return lax.all_to_all(copies, axis, 0, 0).reshape(-1, value.shape[1])


def swap_cores(value):
    return lax.ppermute(value, "core", [(0, 1), (1, 0)])


def body(covariance):
    ny, nz, nx = (lax.axis_size(axis) for axis in ("y", "z", "x"))
    core, x, y, z = (lax.axis_index(axis) for axis in ("core", "x", "y", "z"))
    half = NB // 2
    here = jnp.stack([y * 2 + core, z * nx + x, core, x]).astype(jnp.int32)

    inverse = factor_inverse(covariance)
    mine = pick(core, inverse, swap_cores(inverse[half:]))
    part = send_parts(mine, ("z", "x"), nz * nx)
    part = gather(part, "y", ny)[: part.shape[0]]
    mine = gather(part, ("z", "x"), nz * nx)
    inverse = mine, swap_cores(mine)

    quarter = send_parts(covariance, "x", nx)
    spread = lax.ppermute(quarter, "z", [(0, 3)]) + lax.ppermute(quarter, "z", [(0, 5)])
    spread = jnp.where(z == 0, quarter, spread)
    own = lax.ppermute(spread, "z", [(0, 1), (3, 4), (5, 6)])
    own = own + lax.ppermute(spread, "z", [(0, 7), (3, 2)])
    own = jnp.where((z == 0) | (z == 3) | (z == 5), spread, own)
    ring = [(i, (i + 1) % nx) for i in range(nx)]
    back_ring = [(j, i) for i, j in ring]
    back = lax.ppermute(own, "x", ring)
    ahead = lax.ppermute(own, "x", back_ring)
    rest = own.shape[0] // 2
    top = lax.ppermute(back[:rest], "x", ring)
    low = lax.ppermute(ahead[rest:], "x", back_ring)

    mirror = covariance[:NB]
    for step in (4, 2, 1):
        pairs = [(2 * i, 2 * (i + step)) for i in range(0, ny, 2 * step)]
        sent = lax.ppermute(mirror, ("y", "core"), pairs)
        mirror = jnp.where(y % (2 * step) == step, sent, mirror)
    mirror = mirror, lax.ppermute(mirror, "core", [(0, 1)])
    return update(here, covariance, (own, back, top, low, ahead), mirror, inverse)


def solution(mesh):
    fine = Mesh(mesh.devices.reshape(8, 2, 8, 4), ("y", "core", "z", "x"))
    spec = P(("y", "core"), ("z", "x"))
    return jax.shard_map(body, mesh=fine, in_specs=(spec,), out_specs=spec, check_vma=False)
```

```python
import functools

import jax
import jax.numpy as jnp
from jax import lax
from jax.experimental import pallas as pl
from jax.experimental.pallas import tpu as pltpu
from jax.sharding import Mesh
from jax.sharding import PartitionSpec as P

NB = 512
BK = 128
SUB = 8
CHUNK = 256
HIGH = lax.Precision.HIGHEST


def _rows(value, m):
    return jnp.broadcast_to(value[m : m + 1, :], (SUB, BK))


def _lanes(value, m):
    return jnp.broadcast_to(value[:, m : m + 1], (SUB, BK))


def _small_inverse(rows):
    lane = lax.broadcasted_iota(jnp.int32, (SUB, BK), 1)
    sub = lax.broadcasted_iota(jnp.int32, (SUB, BK), 0)
    rows = list(rows)
    n = len(rows)
    out = []
    for k in range(n):
        base = SUB * k
        pivot = (lane >= base) & (lane < base + SUB)
        p = [_rows(rows[k], m) for m in range(SUB)]
        c = [[_lanes(p[m], base + l) if l >= m else None for l in range(SUB)] for m in range(SUB)]
        p = [
            jnp.where(pivot, jnp.where(lane == base + m, 1.0, 0.0), p[m]) for m in range(SUB)
        ]
        if k + 1 < n:
            g = [_lanes(rows[k + 1], base + m) for m in range(SUB)]
            ahead = jnp.where(pivot, 0.0, rows[k + 1])
        f = [[None] * SUB for _ in range(SUB)]
        inv = []
        for j in range(SUB):
            inv.append(pl.reciprocal(c[j][j], approx=True))
            for l in range(j + 1, SUB):
                f[j][l] = c[j][l] * inv[j]
                for l2 in range(l, SUB):
                    c[l][l2] = c[l][l2] - f[j][l] * c[j][l2]
            for l in range(j + 1, SUB):
                p[l] = p[l] - f[j][l] * p[j]
            if k + 1 < n:
                h = g[j] * inv[j]
                ahead = ahead - h * p[j]
                for l in range(j + 1, SUB):
                    g[l] = g[l] - h * c[j][l]
        done = p[0] * lax.rsqrt(c[0][0])
        for m in range(1, SUB):
            done = jnp.where(sub == m, p[m] * lax.rsqrt(c[m][m]), done)
        out.append(jnp.where(lane <= sub + base, done, 0.0))
        if k + 1 < n:
            rows[k + 1] = ahead
        if k + 2 < n:
            s = [p[m] * inv[m] for m in range(SUB)]
            for l in range(SUB - 1, 0, -1):
                for j in range(l):
                    s[j] = s[j] - f[j][l] * s[l]
            for i in range(k + 2, n):
                parts = [_lanes(rows[i], base + m) * s[m] for m in range(SUB)]
                while len(parts) > 1:
                    parts = [a + b for a, b in zip(parts[::2], parts[1::2])]
                rows[i] = jnp.where(pivot, 0.0, rows[i]) - parts[0]
    return out


def _dot(a, b):
    return lax.dot_general(
        a,
        b,
        (((1,), (0,)), ((), ())),
        precision=HIGH,
        preferred_element_type=jnp.float32,
    )


def _eliminate(k, v_ref):
    here = slice(k * BK, (k + 1) * BK)
    rows = [v_ref[k * BK + SUB * i : k * BK + SUB * (i + 1), here] for i in range(BK // SUB)]
    small = jnp.concatenate(_small_inverse(rows), axis=0)
    v_ref[here, :] = _dot(small, v_ref[here, :])
    v_ref[here, here] = small
    for i in range(k + 1, NB // BK):
        there = slice(i * BK, (i + 1) * BK)
        v_ref[there, here] = jnp.zeros((BK, BK), jnp.float32)
        v_ref[there, :] -= _dot(v_ref[here, there].T, v_ref[here, :])


def _first_kernel(here_ref, mine_ref, other_ref, v_ref):
    half = NB // 2

    @pl.when(here_ref[2] == 0)
    def _():
        v_ref[:half, :] = mine_ref[...]
        v_ref[half:, :] = other_ref[...]

    @pl.when(here_ref[2] != 0)
    def _():
        v_ref[:half, :] = other_ref[...]
        v_ref[half:, :] = mine_ref[...]

    _eliminate(0, v_ref)


def _next_kernel(k, old_ref, v_ref):
    v_ref[...] = old_ref[...]
    _eliminate(k, v_ref)


def factor_inverse(here, mine, other):
    vmem = pl.BlockSpec(memory_space=pltpu.VMEM)
    rest = dict(
        out_shape=jax.ShapeDtypeStruct((NB, NB), jnp.float32),
        out_specs=vmem,
        compiler_params=pltpu.CompilerParams(vmem_limit_bytes=24 * 2**20),
        cost_estimate=pl.CostEstimate(flops=10**6, bytes_accessed=10**5, transcendentals=NB),
    )
    state = pl.pallas_call(
        _first_kernel,
        in_specs=[pl.BlockSpec(memory_space=pltpu.SMEM), vmem, vmem],
        name="factor_0",
        **rest,
    )(here, mine, other)
    for k in range(1, NB // BK):
        state = pl.pallas_call(
            functools.partial(_next_kernel, k), in_specs=[vmem], name=f"factor_{k}", **rest
        )(state)
    return state


def _pick_kernel(which_ref, first_ref, *refs):
    *others, _, o_ref, sem = refs
    for i, ref in enumerate((first_ref.at[: o_ref.shape[0]], *others)):

        @pl.when(which_ref[0] == i)
        def _():
            copy = pltpu.make_async_copy(ref, o_ref, sem)
            copy.start()
            copy.wait()


def pick(which, first, *others, after):
    return pl.pallas_call(
        _pick_kernel,
        out_shape=jax.ShapeDtypeStruct(others[0].shape, jnp.float32),
        in_specs=[pl.BlockSpec(memory_space=pltpu.SMEM)]
        + [pl.BlockSpec(memory_space=pl.ANY)] * (2 + len(others)),
        out_specs=pl.BlockSpec(memory_space=pltpu.VMEM),
        scratch_shapes=[pltpu.SemaphoreType.DMA],
        cost_estimate=pl.CostEstimate(flops=0, bytes_accessed=10**6, transcendentals=0),
        name="pick",
    )(which.reshape(1), first, *others, after)


def _split(value):
    top = value.astype(jnp.bfloat16)
    return top, (value - top.astype(jnp.float32)).astype(jnp.bfloat16)


def _dot3(a, b, dims):
    return sum(
        lax.dot_general(x, y, (dims, ((), ())), preferred_element_type=jnp.float32)
        for x, y in ((a[1], b[0]), (a[0], b[1]), (a[0], b[0]))
    )


def _update_kernel(
    here_ref, state_ref, panel_ref, tile_ref, sent_ref, inverse_ref,
    o_ref, whole_ref, inv_ref, mirror_ref, sem,
):
    row, col, core = (here_ref[j] for j in range(3))
    i = pl.program_id(0)
    first = pl.multiple_of(i * CHUNK, CHUNK)

    @pl.when(i == 0)
    def _():
        for value, ref in ((0, tile_ref), (1, sent_ref)):

            @pl.when(core == value)
            def _():
                copy = pltpu.make_async_copy(ref, whole_ref, sem)
                copy.start()
                copy.wait()

        for k in range(NB // BK):
            here = slice(k * BK, (k + 1) * BK)
            wide = inverse_ref[here, :]
            lane = lax.broadcasted_iota(jnp.int32, wide.shape, 1)
            top, low = _split(jnp.where(lane < (k + 1) * BK, wide, 0.0))
            inv_ref[0, here, :] = top
            inv_ref[1, here, :] = low
        mirror = _split(_dot3((inv_ref[0], inv_ref[1]), _split(whole_ref[...]), ((1,), (0,))))
        mirror_ref[0] = mirror[0]
        mirror_ref[1] = mirror[1]

    solved = _dot3(_split(panel_ref[...]), (inv_ref[0], inv_ref[1]), ((1,), (1,)))
    top = (row == 0) & (first < NB)

    @pl.when(col == 0)
    def _():
        r = lax.broadcasted_iota(jnp.int32, solved.shape, 0) + first
        c = lax.broadcasted_iota(jnp.int32, solved.shape, 1)
        o_ref[...] = jnp.where(top & (c > r), 0.0, solved)

    @pl.when(col != 0)
    def _():
        new = state_ref[...] - _dot3(_split(solved), (mirror_ref[0], mirror_ref[1]), ((1,), (0,)))
        o_ref[...] = jnp.where(top, 0.0, new)


def update(here, state, panel, mirror, inverse):
    block = pl.BlockSpec((CHUNK, NB), lambda i: (i, 0))
    tile = pl.BlockSpec((NB, NB), lambda i: (0, 0))
    return pl.pallas_call(
        _update_kernel,
        grid=(state.shape[0] // CHUNK,),
        out_shape=jax.ShapeDtypeStruct(state.shape, jnp.float32),
        in_specs=[pl.BlockSpec(memory_space=pltpu.SMEM), block, block]
        + [pl.BlockSpec(memory_space=pl.ANY)] * 2
        + [tile],
        out_specs=block,
        scratch_shapes=[
            pltpu.VMEM((NB, NB), jnp.float32),
            pltpu.VMEM((2, NB, NB), jnp.bfloat16),
            pltpu.VMEM((2, NB, NB), jnp.bfloat16),
            pltpu.SemaphoreType.DMA,
        ],
        compiler_params=pltpu.CompilerParams(vmem_limit_bytes=40 * 2**20),
        cost_estimate=pl.CostEstimate(
            flops=30 * NB**3, bytes_accessed=32 * NB * NB, transcendentals=0
        ),
        name="update",
    )(here, state, panel, *mirror, inverse)


def send_parts(value, axis, parts):
    size = value.shape[0] // parts
    return lax.all_to_all(value.reshape(parts, size, value.shape[1]), axis, 0, 0)[0]


def gather(value, axis, parts):
    copies = jnp.broadcast_to(value[None], (parts,) + value.shape)
    return lax.all_to_all(copies, axis, 0, 0).reshape(-1, value.shape[1])


def swap_cores(value):
    return lax.ppermute(value, "core", [(0, 1), (1, 0)])


def body(covariance):
    ny, nz, nx = (lax.axis_size(axis) for axis in ("y", "z", "x"))
    core, x, y, z = (lax.axis_index(axis) for axis in ("core", "x", "y", "z"))
    half = NB // 2
    here = jnp.stack([y * 2 + core, z * nx + x, core]).astype(jnp.int32)

    quarter = send_parts(covariance, "x", nx)
    spread = lax.ppermute(quarter, "z", [(0, 3)]) + lax.ppermute(quarter, "z", [(0, 5)])
    spread = jnp.where(z == 0, quarter, spread)
    own = lax.ppermute(spread, "z", [(0, 1), (3, 4), (5, 6)])
    own = own + lax.ppermute(spread, "z", [(0, 7), (3, 2)])
    own = jnp.where((z == 0) | (z == 3) | (z == 5), spread, own)
    panel = gather(own, "x", nx)

    mine = pick(core, covariance, swap_cores(covariance[half:NB]), after=quarter)
    part = send_parts(mine, ("z", "x"), nz * nx)
    part = gather(part, "y", ny)[: part.shape[0]]
    diagonal = gather(part, ("z", "x"), nz * nx)
    inverse = factor_inverse(here, diagonal, swap_cores(diagonal))

    mirror = covariance[:NB]
    for step in (4, 2, 1):
        pairs = [(2 * i, 2 * (i + step)) for i in range(0, ny, 2 * step)]
        sent = lax.ppermute(mirror, ("y", "core"), pairs)
        mirror = jnp.where(y % (2 * step) == step, sent, mirror)
    mirror = mirror, lax.ppermute(mirror, "core", [(0, 1)])
    return update(here, covariance, panel, mirror, inverse)


def solution(mesh):
    fine = Mesh(mesh.devices.reshape(8, 2, 8, 4), ("y", "core", "z", "x"))
    spec = P(("y", "core"), ("z", "x"))
    return jax.shard_map(body, mesh=fine, in_specs=(spec,), out_specs=spec, check_vma=False)
```

```python
import functools

import jax
import jax.numpy as jnp
from jax import lax
from jax.experimental import pallas as pl
from jax.experimental.pallas import tpu as pltpu
from jax.sharding import Mesh
from jax.sharding import PartitionSpec as P

NB = 512
BK = 128
SUB = 8
CHUNK = 256
HIGH = lax.Precision.HIGHEST


def _rows(value, m):
    return jnp.broadcast_to(value[m : m + 1, :], (SUB, BK))


def _lanes(value, m):
    return jnp.broadcast_to(value[:, m : m + 1], (SUB, BK))


def _small_inverse(rows):
    lane = lax.broadcasted_iota(jnp.int32, (SUB, BK), 1)
    sub = lax.broadcasted_iota(jnp.int32, (SUB, BK), 0)
    rows = list(rows)
    n = len(rows)
    out = []
    for k in range(n):
        base = SUB * k
        pivot = (lane >= base) & (lane < base + SUB)
        p = [_rows(rows[k], m) for m in range(SUB)]
        c = [[_lanes(p[m], base + l) if l >= m else None for l in range(SUB)] for m in range(SUB)]
        p = [
            jnp.where(pivot, jnp.where(lane == base + m, 1.0, 0.0), p[m]) for m in range(SUB)
        ]
        if k + 1 < n:
            g = [_lanes(rows[k + 1], base + m) for m in range(SUB)]
            ahead = jnp.where(pivot, 0.0, rows[k + 1])
        f = [[None] * SUB for _ in range(SUB)]
        inv = []
        for j in range(SUB):
            inv.append(pl.reciprocal(c[j][j], approx=True))
            for l in range(j + 1, SUB):
                f[j][l] = c[j][l] * inv[j]
                for l2 in range(l, SUB):
                    c[l][l2] = c[l][l2] - f[j][l] * c[j][l2]
            for l in range(j + 1, SUB):
                p[l] = p[l] - f[j][l] * p[j]
            if k + 1 < n:
                h = g[j] * inv[j]
                ahead = ahead - h * p[j]
                for l in range(j + 1, SUB):
                    g[l] = g[l] - h * c[j][l]
        done = p[0] * lax.rsqrt(c[0][0])
        for m in range(1, SUB):
            done = jnp.where(sub == m, p[m] * lax.rsqrt(c[m][m]), done)
        out.append(jnp.where(lane <= sub + base, done, 0.0))
        if k + 1 < n:
            rows[k + 1] = ahead
        if k + 2 < n:
            s = [p[m] * inv[m] for m in range(SUB)]
            for l in range(SUB - 1, 0, -1):
                for j in range(l):
                    s[j] = s[j] - f[j][l] * s[l]
            for i in range(k + 2, n):
                parts = [_lanes(rows[i], base + m) * s[m] for m in range(SUB)]
                while len(parts) > 1:
                    parts = [a + b for a, b in zip(parts[::2], parts[1::2])]
                rows[i] = jnp.where(pivot, 0.0, rows[i]) - parts[0]
    return out


def _dot(a, b):
    return lax.dot_general(
        a,
        b,
        (((1,), (0,)), ((), ())),
        precision=HIGH,
        preferred_element_type=jnp.float32,
    )


def _eliminate(k, v_ref):
    here = slice(k * BK, (k + 1) * BK)
    rows = [v_ref[k * BK + SUB * i : k * BK + SUB * (i + 1), here] for i in range(BK // SUB)]
    small = jnp.concatenate(_small_inverse(rows), axis=0)
    v_ref[here, :] = _dot(small, v_ref[here, :])
    v_ref[here, here] = small
    for i in range(k + 1, NB // BK):
        there = slice(i * BK, (i + 1) * BK)
        v_ref[there, here] = jnp.zeros((BK, BK), jnp.float32)
        v_ref[there, :] -= _dot(v_ref[here, there].T, v_ref[here, :])


def _factor_kernel(k, old_ref, *refs):
    v_ref = refs[-1]
    v_ref[...] = old_ref[...]
    _eliminate(k, v_ref)


def _last_kernel(old_ref, upper_ref, lower_ref, v_ref):
    _factor_kernel(NB // BK - 1, old_ref, v_ref)
    upper_ref[...] = v_ref[: NB // 2, :]
    lower_ref[...] = v_ref[NB // 2 :, :]


def factor_inverse(covariance, after):
    state = covariance
    whole = pl.BlockSpec((NB, NB), lambda i: (0, 0))
    half = pl.BlockSpec((NB // 2, NB), lambda i: (0, 0))
    rest = dict(
        grid=(1,),
        compiler_params=pltpu.CompilerParams(vmem_limit_bytes=24 * 2**20),
        cost_estimate=pl.CostEstimate(flops=10**6, bytes_accessed=10**5, transcendentals=NB),
    )
    for k in range(NB // BK - 1):
        extra = (after,) if k == 2 else ()
        state = pl.pallas_call(
            functools.partial(_factor_kernel, k),
            out_shape=jax.ShapeDtypeStruct((NB, NB), jnp.float32),
            in_specs=[whole] + [pl.BlockSpec(memory_space=pl.ANY)] * len(extra),
            out_specs=whole,
            name=f"factor_{k}",
            **rest,
        )(state, *extra)
    return pl.pallas_call(
        _last_kernel,
        out_shape=[jax.ShapeDtypeStruct((NB // 2, NB), jnp.float32)] * 2,
        in_specs=[whole],
        out_specs=[half, half],
        scratch_shapes=[pltpu.VMEM((NB, NB), jnp.float32)],
        name="factor_3",
        **rest,
    )(state)


def _pick_kernel(count, which_ref, *refs):
    *_, o_ref, sem = refs
    for i, ref in enumerate(refs[:count]):

        @pl.when(which_ref[0] == i)
        def _():
            copy = pltpu.make_async_copy(ref, o_ref, sem)
            copy.start()
            copy.wait()


def pick(which, arrays, after):
    operands = (*arrays, *after)
    return pl.pallas_call(
        functools.partial(_pick_kernel, len(arrays)),
        out_shape=jax.ShapeDtypeStruct(arrays[0].shape, jnp.float32),
        in_specs=[pl.BlockSpec(memory_space=pltpu.SMEM)]
        + [pl.BlockSpec(memory_space=pl.ANY)] * len(operands),
        out_specs=pl.BlockSpec(memory_space=pltpu.VMEM),
        scratch_shapes=[pltpu.SemaphoreType.DMA],
        cost_estimate=pl.CostEstimate(flops=0, bytes_accessed=10**6, transcendentals=0),
        name="pick",
    )(which.reshape(1), *operands)


def _split(value):
    top = value.astype(jnp.bfloat16)
    return top, (value - top.astype(jnp.float32)).astype(jnp.bfloat16)


def _dot3(a, b, dims):
    return sum(
        lax.dot_general(x, y, (dims, ((), ())), preferred_element_type=jnp.float32)
        for x, y in ((a[1], b[0]), (a[0], b[1]), (a[0], b[0]))
    )


def _update_kernel(
    here_ref, state_ref, own_ref, back_ref, top_ref, low_ref, ahead_ref, tile_ref, sent_ref,
    mine_ref, other_ref, o_ref, panel_ref, whole_ref, inv_ref, mirror_ref, sem,
):
    row, col, core, x = (here_ref[j] for j in range(4))
    i = pl.program_id(0)
    first = pl.multiple_of(i * CHUNK, CHUNK)
    half = CHUNK // 2

    @pl.when(i == 0)
    def _():
        for value, ref in ((0, tile_ref), (1, sent_ref)):

            @pl.when(core == value)
            def _():
                copy = pltpu.make_async_copy(ref, whole_ref, sem)
                copy.start()
                copy.wait()

        tile = _split(whole_ref[...])
        for value, parts in ((0, (mine_ref, other_ref)), (1, (other_ref, mine_ref))):

            @pl.when(core == value)
            def _():
                for k in range(NB // BK):
                    here = slice(k * BK, (k + 1) * BK)
                    wide = parts[k // 2][(k % 2) * BK : (k % 2 + 1) * BK, :]
                    lane = lax.broadcasted_iota(jnp.int32, wide.shape, 1)
                    top, low = _split(jnp.where(lane < (k + 1) * BK, wide, 0.0))
                    inv_ref[0, here, :] = top
                    inv_ref[1, here, :] = low

        mirror = _split(_dot3((inv_ref[0], inv_ref[1]), tile, ((1,), (0,))))
        mirror_ref[0] = mirror[0]
        mirror_ref[1] = mirror[1]

    turn = lax.rem(x + 4 - i, 4)
    for j, part in ((0, own_ref), (1, back_ref), (3, ahead_ref)):

        @pl.when(turn == j)
        def _():
            panel_ref[...] = part[...]

    @pl.when(turn == 2)
    def _():
        panel_ref[:half, :] = top_ref[...]
        panel_ref[half:, :] = low_ref[...]

    solved = _dot3(_split(panel_ref[...]), (inv_ref[0], inv_ref[1]), ((1,), (1,)))
    top = (row == 0) & (first < NB)

    @pl.when(col == 0)
    def _():
        r = lax.broadcasted_iota(jnp.int32, solved.shape, 0) + first
        c = lax.broadcasted_iota(jnp.int32, solved.shape, 1)
        o_ref[...] = jnp.where(top & (c > r), 0.0, solved)

    @pl.when(col != 0)
    def _():
        new = state_ref[...] - _dot3(_split(solved), (mirror_ref[0], mirror_ref[1]), ((1,), (0,)))
        o_ref[...] = jnp.where(top, 0.0, new)


def update(here, state, panel, mirror, inverse):
    block = pl.BlockSpec((CHUNK, NB), lambda i: (i, 0))
    vmem = pl.BlockSpec(memory_space=pltpu.VMEM)
    anywhere = pl.BlockSpec(memory_space=pl.ANY)
    return pl.pallas_call(
        _update_kernel,
        grid=(state.shape[0] // CHUNK,),
        out_shape=jax.ShapeDtypeStruct(state.shape, jnp.float32),
        in_specs=[pl.BlockSpec(memory_space=pltpu.SMEM), block]
        + [vmem] * 5
        + [anywhere] * 2
        + [vmem] * 2,
        out_specs=block,
        scratch_shapes=[
            pltpu.VMEM((CHUNK, NB), jnp.float32),
            pltpu.VMEM((NB, NB), jnp.float32),
            pltpu.VMEM((2, NB, NB), jnp.bfloat16),
            pltpu.VMEM((2, NB, NB), jnp.bfloat16),
            pltpu.SemaphoreType.DMA,
        ],
        compiler_params=pltpu.CompilerParams(vmem_limit_bytes=40 * 2**20),
        cost_estimate=pl.CostEstimate(
            flops=30 * NB**3, bytes_accessed=32 * NB * NB, transcendentals=0
        ),
        name="update",
    )(here, state, *panel, *mirror, *inverse)


def send_parts(value, axis, parts):
    size = value.shape[0] // parts
    return lax.all_to_all(value.reshape(parts, size, value.shape[1]), axis, 0, 0)[0]


def gather(value, axis, parts):
    copies = jnp.broadcast_to(value[None], (parts,) + value.shape)
    return lax.all_to_all(copies, axis, 0, 0).reshape(-1, value.shape[1])


def swap_cores(value):
    return lax.ppermute(value, "core", [(0, 1), (1, 0)])


def body(covariance):
    ny, nz, nx = (lax.axis_size(axis) for axis in ("y", "z", "x"))
    core, x, y, z = (lax.axis_index(axis) for axis in ("core", "x", "y", "z"))
    here = jnp.stack([y * 2 + core, z * nx + x, core, x]).astype(jnp.int32)

    mirror = covariance[:NB]
    rounds = []
    for step in (4, 2, 1):
        pairs = [(2 * i, 2 * (i + step)) for i in range(0, ny, 2 * step)]
        sent = lax.ppermute(mirror, ("y", "core"), pairs)
        mirror = jnp.where(y % (2 * step) == step, sent, mirror)
        rounds.append(mirror)
    mirror = mirror, lax.ppermute(mirror, "core", [(0, 1)])

    quarter = send_parts(covariance, "x", nx)
    third = lax.ppermute(quarter, "z", [(0, 3)])
    fifth = lax.ppermute(quarter, "z", [(0, 5)])
    spread = jnp.where(z == 0, quarter, third + fifth)
    own = lax.ppermute(spread, "z", [(0, 1), (3, 4), (5, 6)])
    own = own + lax.ppermute(spread, "z", [(0, 7), (3, 2)])
    own = jnp.where((z == 0) | (z == 3) | (z == 5), spread, own)
    ring = [(i, (i + 1) % nx) for i in range(nx)]
    back_ring = [(j, i) for i, j in ring]
    back = lax.ppermute(own, "x", ring)
    ahead = lax.ppermute(own, "x", back_ring)
    rest = own.shape[0] // 2
    top = lax.ppermute(back[:rest], "x", ring)
    low = lax.ppermute(ahead[rest:], "x", back_ring)

    upper, lower = factor_inverse(covariance, rounds[0])
    mine = pick(core, (upper, swap_cores(lower)), (third, fifth))
    part = send_parts(mine, ("z", "x"), nz * nx)
    part = gather(part, "y", ny)[: part.shape[0]]
    mine = gather(part, ("z", "x"), nz * nx)
    inverse = mine, swap_cores(mine)
    return update(here, covariance, (own, back, top, low, ahead), mirror, inverse)


def solution(mesh):
    fine = Mesh(mesh.devices.reshape(8, 2, 8, 4), ("y", "core", "z", "x"))
    spec = P(("y", "core"), ("z", "x"))
    return jax.shard_map(body, mesh=fine, in_specs=(spec,), out_specs=spec, check_vma=False)
```

```python
import functools

import jax
import jax.numpy as jnp
from jax import lax
from jax.experimental import pallas as pl
from jax.experimental.pallas import tpu as pltpu
from jax.sharding import Mesh
from jax.sharding import PartitionSpec as P

NB = 512
BK = 128
SUB = 8
CHUNK = 256
HIGH = lax.Precision.HIGHEST


def _rows(value, m):
    return jnp.broadcast_to(value[m : m + 1, :], (SUB, BK))


def _lanes(value, m):
    return jnp.broadcast_to(value[:, m : m + 1], (SUB, BK))


def _small_inverse(rows):
    lane = lax.broadcasted_iota(jnp.int32, (SUB, BK), 1)
    sub = lax.broadcasted_iota(jnp.int32, (SUB, BK), 0)
    rows = list(rows)
    n = len(rows)
    out = []
    for k in range(n):
        base = SUB * k
        pivot = (lane >= base) & (lane < base + SUB)
        p = [_rows(rows[k], m) for m in range(SUB)]
        c = [[_lanes(p[m], base + l) if l >= m else None for l in range(SUB)] for m in range(SUB)]
        p = [
            jnp.where(pivot, jnp.where(lane == base + m, 1.0, 0.0), p[m]) for m in range(SUB)
        ]
        if k + 1 < n:
            g = [_lanes(rows[k + 1], base + m) for m in range(SUB)]
            ahead = jnp.where(pivot, 0.0, rows[k + 1])
        f = [[None] * SUB for _ in range(SUB)]
        inv = []
        for j in range(SUB):
            inv.append(pl.reciprocal(c[j][j], approx=True))
            for l in range(j + 1, SUB):
                f[j][l] = c[j][l] * inv[j]
                for l2 in range(l, SUB):
                    c[l][l2] = c[l][l2] - f[j][l] * c[j][l2]
            for l in range(j + 1, SUB):
                p[l] = p[l] - f[j][l] * p[j]
            if k + 1 < n:
                h = g[j] * inv[j]
                ahead = ahead - h * p[j]
                for l in range(j + 1, SUB):
                    g[l] = g[l] - h * c[j][l]
        done = p[0] * lax.rsqrt(c[0][0])
        for m in range(1, SUB):
            done = jnp.where(sub == m, p[m] * lax.rsqrt(c[m][m]), done)
        out.append(jnp.where(lane <= sub + base, done, 0.0))
        if k + 1 < n:
            rows[k + 1] = ahead
        if k + 2 < n:
            s = [p[m] * inv[m] for m in range(SUB)]
            for l in range(SUB - 1, 0, -1):
                for j in range(l):
                    s[j] = s[j] - f[j][l] * s[l]
            for i in range(k + 2, n):
                parts = [_lanes(rows[i], base + m) * s[m] for m in range(SUB)]
                while len(parts) > 1:
                    parts = [a + b for a, b in zip(parts[::2], parts[1::2])]
                rows[i] = jnp.where(pivot, 0.0, rows[i]) - parts[0]
    return out


def _dot(a, b):
    return lax.dot_general(
        a,
        b,
        (((1,), (0,)), ((), ())),
        precision=HIGH,
        preferred_element_type=jnp.float32,
    )


def _eliminate(k, v_ref):
    here = slice(k * BK, (k + 1) * BK)
    rows = [v_ref[k * BK + SUB * i : k * BK + SUB * (i + 1), here] for i in range(BK // SUB)]
    small = jnp.concatenate(_small_inverse(rows), axis=0)
    v_ref[here, :] = _dot(small, v_ref[here, :])
    v_ref[here, here] = small
    for i in range(k + 1, NB // BK):
        there = slice(i * BK, (i + 1) * BK)
        v_ref[there, here] = jnp.zeros((BK, BK), jnp.float32)
        v_ref[there, :] -= _dot(v_ref[here, there].T, v_ref[here, :])


def _first_kernel(here_ref, old_ref, sent_ref, v_ref):
    for value, ref in ((0, old_ref), (1, sent_ref)):

        @pl.when(here_ref[2] == value)
        def _():
            v_ref[...] = ref[...]

    _eliminate(0, v_ref)


def _next_kernel(k, old_ref, v_ref):
    v_ref[...] = old_ref[...]
    _eliminate(k, v_ref)


def _last_kernel(here_ref, old_ref, o_ref, v_ref):
    _next_kernel(NB // BK - 1, old_ref, v_ref)
    half = NB // 2
    for value in range(2):

        @pl.when(here_ref[2] == value)
        def _():
            o_ref[...] = v_ref[value * half : (value + 1) * half, :]


def factor_inverse(here, covariance, sent):
    whole = pl.BlockSpec((NB, NB), lambda i: (0, 0))
    half = pl.BlockSpec((NB // 2, NB), lambda i: (0, 0))
    scalars = pl.BlockSpec(memory_space=pltpu.SMEM)
    rest = dict(
        grid=(1,),
        compiler_params=pltpu.CompilerParams(vmem_limit_bytes=24 * 2**20),
        cost_estimate=pl.CostEstimate(flops=10**6, bytes_accessed=10**5, transcendentals=NB),
    )
    tile = jax.ShapeDtypeStruct((NB, NB), jnp.float32)
    state = pl.pallas_call(
        _first_kernel,
        out_shape=tile,
        in_specs=[scalars, whole, whole],
        out_specs=whole,
        name="factor_0",
        **rest,
    )(here, covariance, sent)
    for k in range(1, NB // BK - 1):
        state = pl.pallas_call(
            functools.partial(_next_kernel, k),
            out_shape=tile,
            in_specs=[whole],
            out_specs=whole,
            name=f"factor_{k}",
            **rest,
        )(state)
    return pl.pallas_call(
        _last_kernel,
        out_shape=jax.ShapeDtypeStruct((NB // 2, NB), jnp.float32),
        in_specs=[scalars, whole],
        out_specs=half,
        scratch_shapes=[pltpu.VMEM((NB, NB), jnp.float32)],
        name="factor_3",
        **rest,
    )(here, state)


def _pick_kernel(which_ref, first_ref, second_ref, _, o_ref, sem):
    for i, ref in enumerate((first_ref, second_ref)):

        @pl.when(which_ref[0] == i)
        def _():
            copy = pltpu.make_async_copy(ref, o_ref, sem)
            copy.start()
            copy.wait()


def pick(which, first, second, after):
    return pl.pallas_call(
        _pick_kernel,
        out_shape=jax.ShapeDtypeStruct(first.shape, jnp.float32),
        in_specs=[pl.BlockSpec(memory_space=pltpu.SMEM)]
        + [pl.BlockSpec(memory_space=pl.ANY)] * 3,
        out_specs=pl.BlockSpec(memory_space=pltpu.VMEM),
        scratch_shapes=[pltpu.SemaphoreType.DMA],
        cost_estimate=pl.CostEstimate(flops=0, bytes_accessed=10**6, transcendentals=0),
        name="pick",
    )(which.reshape(1), first, second, after)


def _split(value):
    top = value.astype(jnp.bfloat16)
    return top, (value - top.astype(jnp.float32)).astype(jnp.bfloat16)


def _dot3(a, b, dims):
    return sum(
        lax.dot_general(x, y, (dims, ((), ())), preferred_element_type=jnp.float32)
        for x, y in ((a[1], b[0]), (a[0], b[1]), (a[0], b[0]))
    )


def _update_kernel(
    here_ref, state_ref, own_ref, back_ref, top_ref, low_ref, ahead_ref, tile_ref, sent_ref,
    mine_ref, other_ref, o_ref, panel_ref, whole_ref, inv_ref, mirror_ref, sem,
):
    row, col, core, x = (here_ref[j] for j in range(4))
    i = pl.program_id(0)
    first = pl.multiple_of(i * CHUNK, CHUNK)
    half = CHUNK // 2

    @pl.when(i == 0)
    def _():
        for value, ref in ((0, tile_ref), (1, sent_ref)):

            @pl.when(core == value)
            def _():
                copy = pltpu.make_async_copy(ref, whole_ref, sem)
                copy.start()
                copy.wait()

        tile = _split(whole_ref[...])
        for value, parts in ((0, (mine_ref, other_ref)), (1, (other_ref, mine_ref))):

            @pl.when(core == value)
            def _():
                for k in range(NB // BK):
                    here = slice(k * BK, (k + 1) * BK)
                    wide = parts[k // 2][(k % 2) * BK : (k % 2 + 1) * BK, :]
                    lane = lax.broadcasted_iota(jnp.int32, wide.shape, 1)
                    top, low = _split(jnp.where(lane < (k + 1) * BK, wide, 0.0))
                    inv_ref[0, here, :] = top
                    inv_ref[1, here, :] = low

        mirror = _split(_dot3((inv_ref[0], inv_ref[1]), tile, ((1,), (0,))))
        mirror_ref[0] = mirror[0]
        mirror_ref[1] = mirror[1]

    turn = lax.rem(x + 4 - i, 4)
    for j, part in ((0, own_ref), (1, back_ref), (3, ahead_ref)):

        @pl.when(turn == j)
        def _():
            panel_ref[...] = part[...]

    @pl.when(turn == 2)
    def _():
        panel_ref[:half, :] = top_ref[...]
        panel_ref[half:, :] = low_ref[...]

    solved = _dot3(_split(panel_ref[...]), (inv_ref[0], inv_ref[1]), ((1,), (1,)))
    top = (row == 0) & (first < NB)

    @pl.when(col == 0)
    def _():
        r = lax.broadcasted_iota(jnp.int32, solved.shape, 0) + first
        c = lax.broadcasted_iota(jnp.int32, solved.shape, 1)
        o_ref[...] = jnp.where(top & (c > r), 0.0, solved)

    @pl.when(col != 0)
    def _():
        new = state_ref[...] - _dot3(_split(solved), (mirror_ref[0], mirror_ref[1]), ((1,), (0,)))
        o_ref[...] = jnp.where(top, 0.0, new)


def update(here, state, panel, mirror, inverse):
    block = pl.BlockSpec((CHUNK, NB), lambda i: (i, 0))
    vmem = pl.BlockSpec(memory_space=pltpu.VMEM)
    anywhere = pl.BlockSpec(memory_space=pl.ANY)
    return pl.pallas_call(
        _update_kernel,
        grid=(state.shape[0] // CHUNK,),
        out_shape=jax.ShapeDtypeStruct(state.shape, jnp.float32),
        in_specs=[pl.BlockSpec(memory_space=pltpu.SMEM), block]
        + [vmem] * 5
        + [anywhere] * 2
        + [vmem] * 2,
        out_specs=block,
        scratch_shapes=[
            pltpu.VMEM((CHUNK, NB), jnp.float32),
            pltpu.VMEM((NB, NB), jnp.float32),
            pltpu.VMEM((2, NB, NB), jnp.bfloat16),
            pltpu.VMEM((2, NB, NB), jnp.bfloat16),
            pltpu.SemaphoreType.DMA,
        ],
        compiler_params=pltpu.CompilerParams(vmem_limit_bytes=40 * 2**20),
        cost_estimate=pl.CostEstimate(
            flops=30 * NB**3, bytes_accessed=32 * NB * NB, transcendentals=0
        ),
        name="update",
    )(here, state, *panel, *mirror, *inverse)


def send_parts(value, axis, parts):
    size = value.shape[0] // parts
    return lax.all_to_all(value.reshape(parts, size, value.shape[1]), axis, 0, 0)[0]


def gather(value, axis, parts):
    copies = jnp.broadcast_to(value[None], (parts,) + value.shape)
    return lax.all_to_all(copies, axis, 0, 0).reshape(-1, value.shape[1])


def swap_cores(value):
    return lax.ppermute(value, "core", [(0, 1), (1, 0)])


def body(covariance):
    ny, nz, nx = (lax.axis_size(axis) for axis in ("y", "z", "x"))
    core, x, y, z = (lax.axis_index(axis) for axis in ("core", "x", "y", "z"))
    here = jnp.stack([y * 2 + core, z * nx + x, core, x]).astype(jnp.int32)

    tile = covariance[:NB]
    mine = half = factor_inverse(here, covariance, lax.ppermute(tile, "core", [(0, 1)]))
    part = send_parts(mine, ("z", "x"), nz * nx)
    part = gather(part, "y", ny)[: part.shape[0]]
    mine = gather(part, ("z", "x"), nz * nx)
    inverse = mine, swap_cores(mine)

    quarter = send_parts(covariance, "x", nx)
    spread = lax.ppermute(quarter, "z", [(0, 3)]) + lax.ppermute(quarter, "z", [(0, 5)])
    spread = jnp.where(z == 0, quarter, spread)
    own = lax.ppermute(spread, "z", [(0, 1), (3, 4), (5, 6)])
    own = own + lax.ppermute(spread, "z", [(0, 7), (3, 2)])
    own = jnp.where((z == 0) | (z == 3) | (z == 5), spread, own)
    ring = [(i, (i + 1) % nx) for i in range(nx)]
    back_ring = [(j, i) for i, j in ring]
    back = lax.ppermute(own, "x", ring)
    ahead = lax.ppermute(own, "x", back_ring)
    rest = own.shape[0] // 2
    top = lax.ppermute(back[:rest], "x", ring)
    low = lax.ppermute(ahead[rest:], "x", back_ring)

    mirror = tile
    for step in (4, 2, 1):
        pairs = [(2 * i, 2 * (i + step)) for i in range(0, ny, 2 * step)]
        sent = lax.ppermute(mirror, ("y", "core"), pairs)
        here_now = y % (2 * step) == step
        if step == 4:
            mirror = pick(here_now.astype(jnp.int32), mirror, sent, after=half)
        else:
            mirror = jnp.where(here_now, sent, mirror)
    mirror = mirror, lax.ppermute(mirror, "core", [(0, 1)])
    return update(here, covariance, (own, back, top, low, ahead), mirror, inverse)


def solution(mesh):
    fine = Mesh(mesh.devices.reshape(8, 2, 8, 4), ("y", "core", "z", "x"))
    spec = P(("y", "core"), ("z", "x"))
    return jax.shard_map(body, mesh=fine, in_specs=(spec,), out_specs=spec, check_vma=False)
```
